32 devices in a mesh: wide: 8 (over y, x, core), narrow: 4 (over z).
Axes of the slice: x: 2, y: 2, z: 4, core: 2. Of those that a mesh axis runs over, the one named last changes fastest.
Arguments:
- control: float32 [64, 512, 1024], P(None, 'wide', 'narrow'), may hold values from -6 to 6
- length_scale: float32 [64], replicated, may hold values from 2 to 8
- modes: float32 [127, 64], replicated, may hold values from -0.75 to 0.75
- jacobian: float32 [128, 127], replicated, may hold values from -0.5 to 0.5
- obs_weight: float32 [128], replicated, may hold values from 0.2 to 5
- departures: float32 [8, 4, 8, 128, 128], P('wide', 'narrow'), may hold values from -6 to 6
- send_cols: int32 [8, 4, 8, 128], P('wide', 'narrow'), may hold values from 0 to 16383
- counts: int32 [8, 4, 8], P('wide', 'narrow'), may hold values from 1 to 128, as said below
Outputs:
- gradient: float32 [64, 512, 1024], P(None, 'wide', 'narrow')
- obs_residual: float32 [8, 4, 8, 128, 128], P('wide', 'narrow')
The draws below stay inside these ranges and needn't reach their ends.
Inputs may be any that keep to these rules, and one draw needn't show every extreme that they name: counts[s, b, o] live slots from the device at longitude tile s and latitude tile b to owner o; in every draw one owner receives 128 from every source. `send_cols`: a local column index of the source device, with latitude varying fastest: i * 256 + j, where i is the local longitude row and j the local latitude column.
All inputs are finite; a program needn't handle non-finite values.
Results may differ from the reference program's by a relative error of at most 0.00008.
Values sent between devices are 32-bit elements; how exact they have to be, the bound alone decides.
A program may use at most 128 MiB of HBM per device.

```python
import math
import jax
import jax.numpy as jnp
from jax import lax

M = 64
L = 127
CH = 128
HALO = 15
LON_DEV = 64
LAT_DEV = 256
CAP = 128
OWNERS = 8
BANDS = 4
NLON = 512
NLAT = 1024


def draw_counts(key, part):
    key = jax.random.fold_in(key, 11)
    first, second, third = jax.random.split(key, 3)
    levels = jax.random.randint(first, (OWNERS,), CAP // 4, CAP + 1)
    drops = jax.random.randint(second, (OWNERS, BANDS, OWNERS), 0, CAP // 4 + 1)
    drawn = jnp.clip(levels[None, None, :] - drops, 1, CAP)
    fullest = jax.random.randint(third, (), 0, OWNERS)
    drawn = jnp.where(jnp.arange(OWNERS)[None, None, :] == fullest, CAP, drawn)
    return drawn.astype(jnp.int32)


def touch_ends(entries, rng, low, largest):
    longest = entries.shape.index(max(entries.shape))
    spots = []
    for shift in (0, 1):
        where = [jax.random.randint(jax.random.fold_in(rng, axis), (), 0, length) for axis, length in enumerate(entries.shape)]
        where[longest] = (where[longest] + shift) % entries.shape[longest]
        spots.append(tuple(where))
    return entries.at[spots[0]].set(low).at[spots[1]].set(largest)


def block_levels(own_key, dims, pieces, low, top_value):
    loudness, own = 1.0, jax.random.fold_in(own_key, 6)
    for position, parts in pieces:
        steps = jnp.exp(jax.random.uniform(jax.random.fold_in(own, position), (parts,), jnp.float32, low / len(pieces), top_value / len(pieces)))
        loudness = loudness * jnp.repeat(steps, dims[position] // parts).reshape([-1 if axis == position else 1 for axis in range(len(dims))])
    return loudness


def centred(own_key, dims, width, bound, cuts=(), kind=jnp.bfloat16):
    values = width * jax.random.normal(own_key, dims, jnp.float32)
    if cuts:
        values = values * block_levels(own_key, dims, cuts, -0.22, 0.18)
    return jnp.clip(values, -bound, bound).astype(kind)


def setup_inputs(seed: int = 0) -> dict:
    keys = jax.random.split(jax.random.key(seed), 9)
    return {
        "control": centred(keys[0], (M, NLON, NLAT), 1.0, 6.0, ((1, 8), (2, 4)), jnp.float32),
        "length_scale": jnp.clip(jnp.exp(jax.random.uniform(keys[1], (M,), jnp.float32, math.log(2.0), math.log(8.0))), 2.0, 8.0),
        "modes": centred(keys[2], (L, M), M ** -0.5, 0.75, (), jnp.float32),
        "jacobian": centred(keys[3], (CH, L), L ** -0.5, 0.5, (), jnp.float32),
        "obs_weight": jnp.clip(jnp.exp(jax.random.uniform(keys[4], (CH,), jnp.float32, math.log(0.2), math.log(5.0))), 0.2, 5.0),
        "departures": centred(keys[5], (OWNERS, BANDS, OWNERS, CH, CAP), 1.0, 6.0, ((0, 8), (1, 4)), jnp.float32),
        "send_cols": touch_ends(jax.random.randint(keys[6], (OWNERS, BANDS, OWNERS, CAP), 0, LON_DEV * LAT_DEV), jax.random.fold_in(keys[6], 1), 0, (LON_DEV * LAT_DEV) - 1).astype(jnp.int32),
        "counts": draw_counts(jax.random.fold_in(keys[8], 71), 0),
    }


def gauss_kernel(length_scale):
    offsets = jnp.arange(-HALO, HALO + 1).astype(jnp.float32)
    curve = jnp.exp(-offsets[None, :] ** 2 / (2.0 * length_scale[:, None] ** 2))
    return curve / jnp.sqrt(lax.optimization_barrier(jnp.sum(curve * curve, axis=1, keepdims=True)))

def filter_axis(field, weights, axis):
    cell_count = field.shape[axis]
    widths = [(0, 0), (0, 0)]
    widths[axis] = (HALO, HALO)
    padded = jnp.pad(field, widths)
    summed = jnp.zeros_like(field)
    for place in range(2 * HALO + 1):
        summed = summed + weights[place] * lax.slice_in_dim(padded, place, place + cell_count, axis=axis)
    return summed

def smooth(field, kernel):

    def one_mode(items):
        plane, weights = items
        return filter_axis(filter_axis(plane, weights, 0), weights, 1)
    return lax.map(one_mode, (field, kernel))

def reference(control, length_scale, modes, jacobian, obs_weight, departures, send_cols, counts):
    highest = lax.Precision.HIGHEST
    kernel = gauss_kernel(length_scale)
    smoothed = smooth(control, kernel)
    source_ids = jnp.arange(OWNERS).astype(jnp.int32)[:, None, None, None]
    band_ids = jnp.arange(BANDS).astype(jnp.int32)[None, :, None, None]
    lon_index = (source_ids * LON_DEV + send_cols // LAT_DEV).astype(jnp.int32)
    lat_index = (band_ids * LAT_DEV + send_cols % LAT_DEV).astype(jnp.int32)
    picked = smoothed[:, lon_index, lat_index]
    profile = jnp.einsum('lm,msnok->lsnok', modes, picked, precision=highest)
    evolved = jnp.einsum('cl,lsnok->onsck', jacobian, profile, precision=highest)
    live_slots = jnp.arange(CAP)[None, None, None, :] < counts[..., None]
    live_slots = jnp.transpose(live_slots, (2, 1, 0, 3))[:, :, :, None, :]
    obs_residual = jnp.where(live_slots, obs_weight[:, None] * (evolved - departures), jnp.float32(0.0))
    adjoint_levels = jnp.einsum('cl,onsck->lsnok', jacobian, obs_residual, precision=highest)
    adjoint_modes = jnp.einsum('lm,lsnok->msnok', modes, adjoint_levels, precision=highest)
    collected = jnp.zeros(control.shape, jnp.float32).at[:, lon_index, lat_index].add(adjoint_modes)
    gradient = control + smooth(collected, kernel)
    return (gradient, obs_residual)
```

```python
import functools

import jax
import jax.numpy as jnp
from jax import lax
from jax.experimental import pallas as pl
from jax.experimental.pallas import tpu as pltpu
from jax.sharding import PartitionSpec as P

HALO = 15
REACH = 16
LANES = 128
STEP = 8
HIGHEST = lax.Precision.HIGHEST
VMEM_BYTES = 48 * 2**20


def split(x):
    high = x.astype(jnp.bfloat16)
    return high, (x - high.astype(jnp.float32)).astype(jnp.bfloat16)


def taps(offset, rate, scale):
    curve = jnp.exp((offset * offset).astype(jnp.float32) * rate) * scale
    return jnp.where(jnp.abs(offset) <= HALO, curve, 0.0)


def lon_kernel(halves, rate_ref, scale_ref, x_ref, before_ref, after_ref, y_ref, first_ref, last_ref):
    lon = y_ref.shape[1]
    depth = lon + 2 * REACH
    row = lax.broadcasted_iota(jnp.int32, (lon, depth), 0)
    col = lax.broadcasted_iota(jnp.int32, (lon, depth), 1)
    offset = col - REACH - row
    lane = lax.broadcasted_iota(jnp.int32, (8, LANES), 1)
    for m in range(STEP):
        mode = pl.program_id(0) * STEP + m
        if halves:
            x = jnp.concatenate([x_ref[0, m], x_ref[1, m]], axis=1)
            before = jnp.concatenate([before_ref[0, m], before_ref[1, m]], axis=1)
            after = jnp.concatenate([after_ref[0, m], after_ref[1, m]], axis=1)
        else:
            x, before, after = x_ref[m], before_ref[m], after_ref[m]
        high, low = split(jnp.concatenate([before, x, after], axis=0))
        w_high, w_low = split(taps(offset, rate_ref[mode], scale_ref[mode]))
        both = jnp.dot(
            jnp.concatenate([w_high, w_low], axis=0), high, preferred_element_type=jnp.float32
        )
        y = both[:lon] + both[lon:]
        y = y + jnp.dot(w_high, low, preferred_element_type=jnp.float32)
        y_ref[m] = y
        width = y.shape[1]
        first = jnp.zeros((8, LANES), jnp.float32)
        last = jnp.zeros((8, LANES), jnp.float32)
        for g in range(lon // 8):
            here = lane // REACH == g
            start = y[8 * g : 8 * g + 8, :LANES]
            end = y[8 * g : 8 * g + 8, width - LANES :]
            if g:
                start = pltpu.roll(start, REACH * g, 1)
            if g < lon // 8 - 1:
                end = pltpu.roll(end, (REACH * g + REACH) % LANES, 1)
            first = jnp.where(here, start, first)
            last = jnp.where(here, end, last)
        first_ref[m] = first
        last_ref[m] = last


def lat_kernel(add, rate_ref, scale_ref, y_ref, before_ref, after_ref, *rest):
    lon, lat = y_ref.shape[1], y_ref.shape[2]
    tiles = lat // LANES
    depth = 2 * LANES
    row = lax.broadcasted_iota(jnp.int32, (depth, LANES), 0)
    col = lax.broadcasted_iota(jnp.int32, (depth, LANES), 1)
    offset = jnp.where(row < 3 * LANES // 2, row, row - depth) - col
    near = lax.broadcasted_iota(jnp.int32, (lon, LANES), 1) < LANES // 2
    out_ref = rest[-1]
    for m in range(STEP):
        mode = pl.program_id(0) * STEP + m
        before, after = before_ref[m], after_ref[m]
        lefts, rights = [], []
        for g in range(lon // 8):
            lefts.append(pltpu.roll(before, LANES - REACH - REACH * g, 1) if g < 7 else before)
            rights.append(pltpu.roll(after, LANES - REACH * g, 1) if g else after)
        blocks = [y_ref[m, :, LANES * t : LANES * t + LANES] for t in range(tiles)]
        around = [jnp.concatenate(lefts, axis=0)] + blocks + [jnp.concatenate(rights, axis=0)]
        sides = [jnp.where(near, around[t + 2], around[t]) for t in range(tiles)]
        field = jnp.concatenate(
            [jnp.concatenate([blocks[t], sides[t]], axis=1) for t in range(tiles)], axis=0
        )
        high, low = split(field)
        w_high, w_low = split(taps(offset, rate_ref[mode], scale_ref[mode]))
        both = jnp.dot(
            jnp.concatenate([high, low], axis=0),
            jnp.concatenate([w_high, w_low], axis=1),
            preferred_element_type=jnp.float32,
        )
        count = tiles * lon
        z = both[:count, :LANES] + both[:count, LANES:] + both[count:, :LANES]
        for t in range(tiles):
            part = z[lon * t : lon * t + lon]
            if add:
                at = slice(LANES * t, LANES * t + LANES)
                out_ref[m, :, at] = rest[0][m, :, at] + part
            else:
                out_ref[t, m * lon : m * lon + lon, :] = part


def observe_kernel(lon, rows_ref, counts_ref, cols_ref, field_ref, normal_ref, offset_ref,
                   picked_ref, collected_ref, table, values):
    modes = normal_ref.shape[0]
    owners, slots = cols_ref.shape

    def to_table(i, carry):
        slab = jnp.concatenate(
            [field_ref[0, pl.ds(i, modes, stride=lon), :], field_ref[1, pl.ds(i, modes, stride=lon), :]],
            axis=0,
        )
        table[pl.ds(pl.multiple_of(i * LANES, LANES), LANES), :] = slab.T
        return carry

    lax.fori_loop(0, lon, to_table, 0, unroll=2)

    def pick(n, carry):
        for u in range(16):
            s = n * 16 + u
            values[pl.ds(s, 1), :] = table[pl.ds(rows_ref[s], 1), :]
        return carry

    lax.fori_loop(0, owners * slots // 16, pick, 0)
    table[...] = jnp.zeros_like(table)
    slot = lax.broadcasted_iota(jnp.int32, (modes, slots), 1)

    def respond(o, carry):
        at = pl.ds(pl.multiple_of(o * slots, slots), slots)
        both = values[at, :].T
        upper = (cols_ref[pl.ds(o, 1), :] & LANES) != 0
        picked = jnp.where(upper, both[modes:], both[:modes])
        count = counts_ref[o]
        picked_ref[o, :modes] = picked
        picked_ref[o, modes:] = jnp.full((8, slots), count.astype(jnp.float32))
        adjoint = jnp.dot(
            normal_ref[...], picked, precision=HIGHEST, preferred_element_type=jnp.float32
        ) - offset_ref[o]
        adjoint = jnp.where(slot < count, adjoint, 0.0)
        values[at, :] = jnp.concatenate(
            [jnp.where(upper, 0.0, adjoint), jnp.where(upper, adjoint, 0.0)], axis=0
        ).T
        return carry

    lax.fori_loop(0, owners, respond, 0)

    def collect(n, carry):
        for u in range(16):
            s = n * 16 + u
            row = rows_ref[s]
            table[pl.ds(row, 1), :] = table[pl.ds(row, 1), :] + values[pl.ds(s, 1), :]
        return carry

    lax.fori_loop(0, owners * slots // 16, collect, 0)

    def from_table(i, carry):
        slab = table[pl.ds(pl.multiple_of(i * LANES, LANES), LANES), :].T
        collected_ref[0, pl.ds(i, modes, stride=lon), :] = slab[:modes]
        collected_ref[1, pl.ds(i, modes, stride=lon), :] = slab[modes:]
        return carry

    lax.fori_loop(0, lon, from_table, 0, unroll=2)


SMEM = pl.BlockSpec(memory_space=pltpu.SMEM)


def by_mode(shape, dim=0):
    block = tuple(STEP if d == dim else n for d, n in enumerate(shape))
    return pl.BlockSpec(block, lambda g: tuple(g if d == dim else 0 for d in range(len(shape))))


def from_neighbours(axis, first, last):
    count = lax.axis_size(axis)
    up = [(i, i + 1) for i in range(count - 1)]
    down = [(j, i) for i, j in up]
    return lax.ppermute(last, axis, up), lax.ppermute(first, axis, down)


def along_lon(x, rate, scale, shape):
    modes, lon, lat = shape
    halves = x.ndim == 4
    dim = x.ndim - 2
    before, after = from_neighbours(
        "wide",
        lax.slice_in_dim(x, 0, REACH, axis=dim),
        lax.slice_in_dim(x, lon - REACH, lon, axis=dim),
    )
    at = 1 if halves else 0
    return pl.pallas_call(
        functools.partial(lon_kernel, halves),
        grid=(modes // STEP,),
        in_specs=[SMEM, SMEM, by_mode(x.shape, at), by_mode(before.shape, at), by_mode(after.shape, at)],
        out_specs=[by_mode(shape), by_mode((modes, 8, LANES)), by_mode((modes, 8, LANES))],
        out_shape=[
            jax.ShapeDtypeStruct(shape, jnp.float32),
            jax.ShapeDtypeStruct((modes, 8, LANES), jnp.float32),
            jax.ShapeDtypeStruct((modes, 8, LANES), jnp.float32),
        ],
        compiler_params=pltpu.CompilerParams(vmem_limit_bytes=VMEM_BYTES),
        name="along_lon",
    )(rate, scale, x, before, after)


def along_lat(y, first, last, rate, scale, added=None):
    modes, lon, lat = y.shape
    before, after = from_neighbours("narrow", first, last)
    extra = () if added is None else (added,)
    if added is None:
        out_shape = (lat // LANES, modes * lon, LANES)
        out_spec = pl.BlockSpec((lat // LANES, STEP * lon, LANES), lambda g: (0, g, 0))
    else:
        out_shape = y.shape
        out_spec = by_mode(y.shape)
    return pl.pallas_call(
        functools.partial(lat_kernel, added is not None),
        grid=(modes // STEP,),
        in_specs=[SMEM, SMEM, by_mode(y.shape), by_mode(before.shape), by_mode(after.shape)]
        + [by_mode(y.shape)] * len(extra),
        out_specs=out_spec,
        out_shape=jax.ShapeDtypeStruct(out_shape, jnp.float32),
        compiler_params=pltpu.CompilerParams(vmem_limit_bytes=VMEM_BYTES),
        name="along_lat",
    )(rate, scale, y, before, after, *extra)


def shards(control, length_scale, modes, jacobian, obs_weight, departures, send_cols, counts):
    owners = lax.axis_size("wide")
    shape = control.shape
    mode_count, lon, lat = shape
    channels = jacobian.shape[0]
    slots = send_cols.shape[-1]
    tiles = lat // LANES

    offsets = jnp.arange(-HALO, HALO + 1).astype(jnp.float32)
    total = jnp.sum(jnp.exp(-(offsets[None, :] ** 2) / length_scale[:, None] ** 2), axis=1)
    rate = -0.5 / (length_scale * length_scale)
    scale = 1.0 / jnp.sqrt(total)

    forward = jnp.dot(jacobian, modes, precision=HIGHEST)
    weighted = obs_weight[:, None] * forward
    normal = jnp.dot(forward.T, weighted, precision=HIGHEST)
    observed = departures.reshape(owners, channels, slots)
    projected = jnp.einsum("cm,sck->smk", weighted, observed, precision=HIGHEST)
    offset = lax.all_to_all(projected, "wide", split_axis=0, concat_axis=0, tiled=True)

    columns = send_cols.reshape(owners, slots)
    rows = ((columns // lat) * LANES + columns % LANES).reshape(-1)

    y, first, last = along_lon(control, rate, scale, shape)
    smoothed = along_lat(y, first, last, rate, scale)
    whole = pl.BlockSpec(memory_space=pltpu.VMEM)
    outgoing, collected = pl.pallas_call(
        functools.partial(observe_kernel, lon),
        in_specs=[SMEM, SMEM] + [whole] * 4,
        out_specs=[whole, whole],
        out_shape=[
            jax.ShapeDtypeStruct((owners, mode_count + 8, slots), jnp.float32),
            jax.ShapeDtypeStruct((tiles, mode_count * lon, LANES), jnp.float32),
        ],
        scratch_shapes=[
            pltpu.VMEM((lon * LANES, LANES), jnp.float32),
            pltpu.VMEM((owners * slots, LANES), jnp.float32),
        ],
        compiler_params=pltpu.CompilerParams(vmem_limit_bytes=VMEM_BYTES),
        name="observe",
    )(rows, counts.reshape(owners), columns, smoothed, normal, offset)

    y, first, last = along_lon(
        collected.reshape(tiles, mode_count, lon, LANES), rate, scale, shape
    )
    arrived = lax.all_to_all(outgoing, "wide", split_axis=0, concat_axis=0, tiled=True)
    gradient = along_lat(y, first, last, rate, scale, control)

    evolved = jnp.einsum("cm,smk->sck", forward, arrived[:, :mode_count], precision=HIGHEST)
    live = jnp.arange(slots).astype(jnp.float32) < arrived[:, mode_count, :]
    residual = jnp.where(
        live[:, None, :], obs_weight[None, :, None] * (evolved - observed), jnp.float32(0.0)
    )
    return (gradient, residual.reshape(departures.shape))


def solution(mesh):
    in_specs = (
        P(None, "wide", "narrow"),
        P(),
        P(),
        P(),
        P(),
        P("wide", "narrow", None, None, None),
        P("wide", "narrow", None, None),
        P("wide", "narrow", None),
    )
    out_specs = (P(None, "wide", "narrow"), P("wide", "narrow", None, None, None))
    return jax.shard_map(shards, mesh=mesh, in_specs=in_specs, out_specs=out_specs, check_vma=False)
```

```python
import functools

import jax
import jax.numpy as jnp
from jax import lax
from jax.experimental import pallas as pl
from jax.experimental.pallas import tpu as pltpu
from jax.sharding import PartitionSpec as P

HALO = 15
REACH = 16
LANES = 128
STEP = 8
LAG = 2
HIGHEST = lax.Precision.HIGHEST
VMEM_BYTES = 48 * 2**20


def split(x):
    high = x.astype(jnp.bfloat16)
    return high, (x - high.astype(jnp.float32)).astype(jnp.bfloat16)


def taps(offset, rate, scale):
    curve = jnp.exp((offset * offset).astype(jnp.float32) * rate) * scale
    return jnp.where(jnp.abs(offset) <= HALO, curve, 0.0)


def lon_filter(halves, mode, rate_ref, scale_ref, x_ref, before_ref, after_ref, y_ref, first_ref, last_ref):
    lon = y_ref.shape[1]
    depth = lon + 2 * REACH
    row = lax.broadcasted_iota(jnp.int32, (lon, depth), 0)
    col = lax.broadcasted_iota(jnp.int32, (lon, depth), 1)
    offset = col - REACH - row
    lane = lax.broadcasted_iota(jnp.int32, (8, LANES), 1)
    if halves:
        x, before, after = (
            jnp.concatenate([ref[0, mode], ref[1, mode]], axis=1)
            for ref in (x_ref, before_ref, after_ref)
        )
    else:
        x, before, after = x_ref[mode], before_ref[mode], after_ref[mode]
    high, low = split(jnp.concatenate([before, x, after], axis=0))
    w_high, w_low = split(taps(offset, rate_ref[mode], scale_ref[mode]))
    both = jnp.dot(
        jnp.concatenate([w_high, w_low], axis=0), high, preferred_element_type=jnp.float32
    )
    y = both[:lon] + both[lon:]
    y = y + jnp.dot(w_high, low, preferred_element_type=jnp.float32)
    y_ref[mode] = y
    width = y.shape[1]
    first = jnp.zeros((8, LANES), jnp.float32)
    last = jnp.zeros((8, LANES), jnp.float32)
    for g in range(lon // 8):
        here = lane // REACH == g
        start = y[8 * g : 8 * g + 8, :LANES]
        end = y[8 * g : 8 * g + 8, width - LANES :]
        if g:
            start = pltpu.roll(start, REACH * g, 1)
        if g < 7:
            end = pltpu.roll(end, REACH * g + REACH, 1)
        first = jnp.where(here, start, first)
        last = jnp.where(here, end, last)
    first_ref[mode] = first
    last_ref[mode] = last


def lat_filter(mode, rate_ref, scale_ref, y_ref, before_ref, after_ref, added_ref, out_ref):
    lon, lat = y_ref.shape[1], y_ref.shape[2]
    tiles = lat // LANES
    depth = 2 * LANES
    row = lax.broadcasted_iota(jnp.int32, (depth, LANES), 0)
    col = lax.broadcasted_iota(jnp.int32, (depth, LANES), 1)
    offset = jnp.where(row < 3 * LANES // 2, row, row - depth) - col
    near = lax.broadcasted_iota(jnp.int32, (lon, LANES), 1) < LANES // 2
    before, after = before_ref[mode], after_ref[mode]
    lefts, rights = [], []
    for g in range(lon // 8):
        lefts.append(pltpu.roll(before, LANES - REACH - REACH * g, 1) if g < 7 else before)
        rights.append(pltpu.roll(after, LANES - REACH * g, 1) if g else after)
    blocks = [y_ref[mode, :, LANES * t : LANES * t + LANES] for t in range(tiles)]
    around = [jnp.concatenate(lefts, axis=0)] + blocks + [jnp.concatenate(rights, axis=0)]
    sides = [jnp.where(near, around[t + 2], around[t]) for t in range(tiles)]
    field = jnp.concatenate(
        [jnp.concatenate([blocks[t], sides[t]], axis=1) for t in range(tiles)], axis=0
    )
    high, low = split(field)
    w_high, w_low = split(taps(offset, rate_ref[mode], scale_ref[mode]))
    both = jnp.dot(
        jnp.concatenate([high, low], axis=0),
        jnp.concatenate([w_high, w_low], axis=1),
        preferred_element_type=jnp.float32,
    )
    count = tiles * lon
    z = both[:count, :LANES] + both[:count, LANES:] + both[count:, :LANES]
    for t in range(tiles):
        part = z[lon * t : lon * t + lon]
        if added_ref is not None:
            at = slice(LANES * t, LANES * t + LANES)
            out_ref[mode, :, at] = added_ref[mode, :, at] + part
        else:
            out_ref[t, mode] = part


def smooth_kernel(halves, add, rate_ref, scale_ref, x_ref, *rest):
    added_ref = rest[0] if add else None
    out_ref, y_ref, before_lon, after_lon, first_lat, last_lat, before_lat, after_lat = rest[add : add + 8]
    send_sems, recv_sems = rest[add + 8 :]
    modes, lon = y_ref.shape[0], y_ref.shape[1]
    chunks = modes // STEP
    axes = ("wide", "narrow")
    spot = [lax.axis_index(axis) for axis in axes]
    size = [lax.axis_size(axis) for axis in axes]
    exists = [spot[0] > 0, spot[0] < size[0] - 1, spot[1] > 0, spot[1] < size[1] - 1]
    target = [{axes[n // 2]: spot[n // 2] + (1 if n % 2 else -1)} for n in range(4)]

    def copy(n, c):
        at = pl.ds(c * STEP, STEP)
        if n < 2:
            rows = pl.ds(lon - REACH, REACH) if n else pl.ds(0, REACH)
            landing = before_lon if n else after_lon
            src = x_ref.at[:, at, rows] if halves else x_ref.at[at, rows]
            dst = landing.at[:, at] if halves else landing.at[at]
        else:
            src = (last_lat if n == 3 else first_lat).at[at]
            dst = (before_lat if n == 3 else after_lat).at[at]
        return pltpu.make_async_remote_copy(
            src_ref=src,
            dst_ref=dst,
            send_sem=send_sems.at[n, c],
            recv_sem=recv_sems.at[n, c],
            device_id=target[n],
            device_id_type=pl.DeviceIdType.MESH,
        )

    barrier = pltpu.get_barrier_semaphore()
    for n in range(4):
        @pl.when(exists[n])
        def _():
            pl.semaphore_signal(
                barrier, inc=1, device_id=target[n], device_id_type=pl.DeviceIdType.MESH
            )
    pl.semaphore_wait(barrier, sum(there.astype(jnp.int32) for there in exists))

    for n in range(2):
        @pl.when(exists[n])
        def _():
            @pl.loop(0, chunks)
            def _(c):
                copy(n, c).start()

    for n, landing in ((1, before_lon), (0, after_lon), (3, before_lat), (2, after_lat)):
        @pl.when(jnp.logical_not(exists[n ^ 1]))
        def _():
            landing[...] = jnp.zeros_like(landing)

    @pl.loop(0, chunks + LAG)
    def _(c):
        @pl.when(c < chunks)
        def _():
            for n in range(2):
                @pl.when(exists[n ^ 1])
                def _():
                    copy(n, c).wait_recv()
            for m in range(STEP):
                lon_filter(
                    halves, c * STEP + m, rate_ref, scale_ref, x_ref, before_lon, after_lon,
                    y_ref, first_lat, last_lat,
                )
            for n in range(2, 4):
                @pl.when(exists[n])
                def _():
                    copy(n, c).start()

        @pl.when(c >= LAG)
        def _():
            done = c - LAG
            for n in range(2, 4):
                @pl.when(exists[n ^ 1])
                def _():
                    copy(n, done).wait_recv()
            for m in range(STEP):
                lat_filter(
                    done * STEP + m, rate_ref, scale_ref, y_ref, before_lat, after_lat, added_ref, out_ref
                )

    for n in range(4):
        @pl.when(exists[n])
        def _():
            @pl.loop(0, chunks)
            def _(c):
                copy(n, c).wait_send()


def observe_kernel(lon, rows_ref, counts_ref, cols_ref, field_ref, normal_ref, offset_ref,
                   picked_ref, collected_ref, table, values):
    modes = normal_ref.shape[0]
    owners, slots = cols_ref.shape

    def to_table(i, carry):
        slab = jnp.concatenate(
            [field_ref[0, pl.ds(i, modes, stride=lon), :], field_ref[1, pl.ds(i, modes, stride=lon), :]],
            axis=0,
        )
        table[pl.ds(pl.multiple_of(i * LANES, LANES), LANES), :] = slab.T
        return carry

    lax.fori_loop(0, lon, to_table, 0, unroll=2)

    def pick(n, carry):
        for u in range(16):
            s = n * 16 + u
            values[pl.ds(s, 1), :] = table[pl.ds(rows_ref[s], 1), :]
        return carry

    lax.fori_loop(0, owners * slots // 16, pick, 0)
    table[...] = jnp.zeros_like(table)
    slot = lax.broadcasted_iota(jnp.int32, (modes, slots), 1)

    def respond(o, carry):
        at = pl.ds(pl.multiple_of(o * slots, slots), slots)
        both = values[at, :].T
        upper = (cols_ref[pl.ds(o, 1), :] & LANES) != 0
        picked = jnp.where(upper, both[modes:], both[:modes])
        count = counts_ref[o]
        picked_ref[o, :modes] = picked
        picked_ref[o, modes:] = jnp.full((8, slots), count.astype(jnp.float32))
        adjoint = jnp.dot(
            normal_ref[...], picked, precision=HIGHEST, preferred_element_type=jnp.float32
        ) - offset_ref[o]
        adjoint = jnp.where(slot < count, adjoint, 0.0)
        values[at, :] = jnp.concatenate(
            [jnp.where(upper, 0.0, adjoint), jnp.where(upper, adjoint, 0.0)], axis=0
        ).T
        return carry

    lax.fori_loop(0, owners, respond, 0)

    def collect(n, carry):
        for u in range(16):
            s = n * 16 + u
            row = rows_ref[s]
            table[pl.ds(row, 1), :] = table[pl.ds(row, 1), :] + values[pl.ds(s, 1), :]
        return carry

    lax.fori_loop(0, owners * slots // 16, collect, 0)

    def from_table(i, carry):
        slab = table[pl.ds(pl.multiple_of(i * LANES, LANES), LANES), :].T
        collected_ref[0, pl.ds(i, modes, stride=lon), :] = slab[:modes]
        collected_ref[1, pl.ds(i, modes, stride=lon), :] = slab[modes:]
        return carry

    lax.fori_loop(0, lon, from_table, 0, unroll=2)


SMEM = pl.BlockSpec(memory_space=pltpu.SMEM)


WHOLE = pl.BlockSpec(memory_space=pltpu.VMEM)


def smooth(x, rate, scale, shape, added=None):
    modes, lon, lat = shape
    halves = x.ndim == 4
    add = added is not None
    landing = (lat // LANES, modes, REACH, LANES) if halves else (modes, REACH, lat)
    out_shape = shape if add else (lat // LANES, modes, lon, LANES)
    return pl.pallas_call(
        functools.partial(smooth_kernel, halves, add),
        in_specs=[SMEM, SMEM, WHOLE] + [WHOLE] * add,
        out_specs=WHOLE,
        out_shape=jax.ShapeDtypeStruct(out_shape, jnp.float32),
        scratch_shapes=[pltpu.VMEM(shape, jnp.float32)]
        + [pltpu.VMEM(landing, jnp.float32)] * 2
        + [pltpu.VMEM((modes, 8, LANES), jnp.float32)] * 4
        + [pltpu.SemaphoreType.DMA((4, modes // STEP))] * 2,
        compiler_params=pltpu.CompilerParams(
            vmem_limit_bytes=VMEM_BYTES, collective_id=int(add), has_side_effects=True
        ),
        name="smooth_add" if add else "smooth",
    )(rate, scale, x, *((added,) if add else ()))


def shards(control, length_scale, modes, jacobian, obs_weight, departures, send_cols, counts):
    owners = lax.axis_size("wide")
    shape = control.shape
    mode_count, lon, lat = shape
    channels = jacobian.shape[0]
    slots = send_cols.shape[-1]
    tiles = lat // LANES

    offsets = jnp.arange(-HALO, HALO + 1).astype(jnp.float32)
    total = jnp.sum(jnp.exp(-(offsets[None, :] ** 2) / length_scale[:, None] ** 2), axis=1)
    rate = -0.5 / (length_scale * length_scale)
    scale = 1.0 / jnp.sqrt(total)

    forward = jnp.dot(jacobian, modes, precision=HIGHEST)
    weighted = obs_weight[:, None] * forward
    normal = jnp.dot(forward.T, weighted, precision=HIGHEST)
    observed = departures.reshape(owners, channels, slots)
    projected = jnp.einsum("cm,sck->smk", weighted, observed, precision=HIGHEST)
    offset = lax.all_to_all(projected, "wide", split_axis=0, concat_axis=0, tiled=True)

    columns = send_cols.reshape(owners, slots)
    rows = ((columns // lat) * LANES + columns % LANES).reshape(-1)

    smoothed = smooth(control, rate, scale, shape).reshape(tiles, mode_count * lon, LANES)
    outgoing, collected = pl.pallas_call(
        functools.partial(observe_kernel, lon),
        in_specs=[SMEM, SMEM] + [WHOLE] * 4,
        out_specs=[WHOLE, WHOLE],
        out_shape=[
            jax.ShapeDtypeStruct((owners, mode_count + 8, slots), jnp.float32),
            jax.ShapeDtypeStruct((tiles, mode_count * lon, LANES), jnp.float32),
        ],
        scratch_shapes=[
            pltpu.VMEM((lon * LANES, LANES), jnp.float32),
            pltpu.VMEM((owners * slots, LANES), jnp.float32),
        ],
        compiler_params=pltpu.CompilerParams(vmem_limit_bytes=VMEM_BYTES),
        name="observe",
    )(rows, counts.reshape(owners), columns, smoothed, normal, offset)

    arrived = lax.all_to_all(outgoing, "wide", split_axis=0, concat_axis=0, tiled=True)
    gradient = smooth(
        collected.reshape(tiles, mode_count, lon, LANES), rate, scale, shape, control
    )

    evolved = jnp.einsum("cm,smk->sck", forward, arrived[:, :mode_count], precision=HIGHEST)
    live = jnp.arange(slots).astype(jnp.float32) < arrived[:, mode_count, :]
    residual = jnp.where(
        live[:, None, :], obs_weight[None, :, None] * (evolved - observed), jnp.float32(0.0)
    )
    return (gradient, residual.reshape(departures.shape))


def solution(mesh):
    in_specs = (
        P(None, "wide", "narrow"),
        P(),
        P(),
        P(),
        P(),
        P("wide", "narrow", None, None, None),
        P("wide", "narrow", None, None),
        P("wide", "narrow", None),
    )
    out_specs = (P(None, "wide", "narrow"), P("wide", "narrow", None, None, None))
    return jax.shard_map(shards, mesh=mesh, in_specs=in_specs, out_specs=out_specs, check_vma=False)
```

```python
import functools

import jax
import jax.numpy as jnp
from jax import lax
from jax.experimental import pallas as pl
from jax.experimental.pallas import tpu as pltpu
from jax.sharding import PartitionSpec as P

HALO = 15
REACH = 16
LANES = 128
STEP = 8
LAG = 2
HIGHEST = lax.Precision.HIGHEST
VMEM_BYTES = 24 * 2**20


def split(x):
    high = x.astype(jnp.bfloat16)
    return high, (x - high.astype(jnp.float32)).astype(jnp.bfloat16)


def taps(offset, rate, scale):
    curve = jnp.exp((offset * offset).astype(jnp.float32) * rate) * scale
    return jnp.where(jnp.abs(offset) <= HALO, curve, 0.0)


def lon_filter(halves, mode, rate_ref, scale_ref, x_ref, before_ref, after_ref, y_ref, first_ref, last_ref):
    lon = y_ref.shape[1]
    depth = lon + 2 * REACH
    row = lax.broadcasted_iota(jnp.int32, (lon, depth), 0)
    col = lax.broadcasted_iota(jnp.int32, (lon, depth), 1)
    offset = col - REACH - row
    lane = lax.broadcasted_iota(jnp.int32, (8, LANES), 1)
    if halves:
        x, before, after = (
            jnp.concatenate([ref[0, mode], ref[1, mode]], axis=1)
            for ref in (x_ref, before_ref, after_ref)
        )
    else:
        x, before, after = x_ref[mode], before_ref[mode], after_ref[mode]
    high, low = split(jnp.concatenate([before, x, after], axis=0))
    w_high, w_low = split(taps(offset, rate_ref[mode], scale_ref[mode]))
    both = jnp.dot(
        jnp.concatenate([w_high, w_low], axis=0), high, preferred_element_type=jnp.float32
    )
    y = both[:lon] + both[lon:]
    y = y + jnp.dot(w_high, low, preferred_element_type=jnp.float32)
    y_ref[mode] = y
    width = y.shape[1]
    first = jnp.zeros((8, LANES), jnp.float32)
    last = jnp.zeros((8, LANES), jnp.float32)
    for g in range(lon // 8):
        here = lane // REACH == g
        start = y[8 * g : 8 * g + 8, :LANES]
        end = y[8 * g : 8 * g + 8, width - LANES :]
        if g:
            start = pltpu.roll(start, REACH * g, 1)
        if g < 7:
            end = pltpu.roll(end, REACH * g + REACH, 1)
        first = jnp.where(here, start, first)
        last = jnp.where(here, end, last)
    first_ref[mode] = first
    last_ref[mode] = last


def lat_filter(mode, rate_ref, scale_ref, y_ref, before_ref, after_ref, out_ref):
    lon, lat = y_ref.shape[1], y_ref.shape[2]
    tiles = lat // LANES
    depth = 2 * LANES
    row = lax.broadcasted_iota(jnp.int32, (depth, LANES), 0)
    col = lax.broadcasted_iota(jnp.int32, (depth, LANES), 1)
    offset = jnp.where(row < 3 * LANES // 2, row, row - depth) - col
    near = lax.broadcasted_iota(jnp.int32, (lon, LANES), 1) < LANES // 2
    before, after = before_ref[mode], after_ref[mode]
    lefts, rights = [], []
    for g in range(lon // 8):
        lefts.append(pltpu.roll(before, LANES - REACH - REACH * g, 1) if g < 7 else before)
        rights.append(pltpu.roll(after, LANES - REACH * g, 1) if g else after)
    blocks = [y_ref[mode, :, LANES * t : LANES * t + LANES] for t in range(tiles)]
    around = [jnp.concatenate(lefts, axis=0)] + blocks + [jnp.concatenate(rights, axis=0)]
    sides = [jnp.where(near, around[t + 2], around[t]) for t in range(tiles)]
    field = jnp.concatenate(
        [jnp.concatenate([blocks[t], sides[t]], axis=1) for t in range(tiles)], axis=0
    )
    high, low = split(field)
    w_high, w_low = split(taps(offset, rate_ref[mode], scale_ref[mode]))
    both = jnp.dot(
        jnp.concatenate([high, low], axis=0),
        jnp.concatenate([w_high, w_low], axis=1),
        preferred_element_type=jnp.float32,
    )
    count = tiles * lon
    z = both[:count, :LANES] + both[:count, LANES:] + both[count:, :LANES]
    for t in range(tiles):
        part = z[lon * t : lon * t + lon]
        if len(out_ref.shape) == 3:
            out_ref[mode, :, LANES * t : LANES * t + LANES] = part
        else:
            out_ref[t, mode] = part


def smooth_kernel(halves, rate_ref, scale_ref, x_ref, parcel_ref, out_ref, arrived_ref, y_ref,
                  before_lon, after_lon, first_lat, last_lat, before_lat, after_lat,
                  send_sems, recv_sems, parcel_send, parcel_recv):
    modes, lon = y_ref.shape[0], y_ref.shape[1]
    chunks = modes // STEP
    axes = ("wide", "narrow")
    spot = [lax.axis_index(axis) for axis in axes]
    size = [lax.axis_size(axis) for axis in axes]
    exists = [spot[0] > 0, spot[0] < size[0] - 1, spot[1] > 0, spot[1] < size[1] - 1]
    target = [{axes[n // 2]: spot[n // 2] + (1 if n % 2 else -1)} for n in range(4)]

    def copy(n, c):
        at = pl.ds(c * STEP, STEP)
        if n < 2:
            rows = pl.ds(lon - REACH, REACH) if n else pl.ds(0, REACH)
            landing = before_lon if n else after_lon
            src = x_ref.at[:, at, rows] if halves else x_ref.at[at, rows]
            dst = landing.at[:, at] if halves else landing.at[at]
        else:
            src = (last_lat if n == 3 else first_lat).at[at]
            dst = (before_lat if n == 3 else after_lat).at[at]
        return pltpu.make_async_remote_copy(
            src_ref=src,
            dst_ref=dst,
            send_sem=send_sems.at[n, c],
            recv_sem=recv_sems.at[n, c],
            device_id=target[n],
            device_id_type=pl.DeviceIdType.MESH,
        )

    def parcel(p):
        peer = lax.rem(spot[0] + p, size[0])
        return pltpu.make_async_remote_copy(
            src_ref=parcel_ref.at[peer],
            dst_ref=arrived_ref.at[spot[0]],
            send_sem=parcel_send.at[p],
            recv_sem=parcel_recv.at[p],
            device_id={"wide": peer},
            device_id_type=pl.DeviceIdType.MESH,
        )

    barrier = pltpu.get_barrier_semaphore()

    @pl.loop(1, size[0])
    def _(p):
        pl.semaphore_signal(
            barrier, inc=1, device_id={"wide": lax.rem(spot[0] + p, size[0])},
            device_id_type=pl.DeviceIdType.MESH,
        )
    for n in range(2, 4):
        @pl.when(exists[n])
        def _():
            pl.semaphore_signal(
                barrier, inc=1, device_id=target[n], device_id_type=pl.DeviceIdType.MESH
            )
    pl.semaphore_wait(barrier, size[0] - 1 + sum(there.astype(jnp.int32) for there in exists[2:]))

    for n in range(2):
        @pl.when(exists[n])
        def _():
            @pl.loop(0, chunks)
            def _(c):
                copy(n, c).start()

    @pl.loop(1, size[0])
    def _(p):
        parcel(p).start()

    arrived_ref[spot[0]] = parcel_ref[spot[0]]

    for n, landing in ((1, before_lon), (0, after_lon), (3, before_lat), (2, after_lat)):
        @pl.when(jnp.logical_not(exists[n ^ 1]))
        def _():
            landing[...] = jnp.zeros_like(landing)

    @pl.loop(0, chunks + LAG)
    def _(c):
        @pl.when(c < chunks)
        def _():
            for n in range(2):
                @pl.when(exists[n ^ 1])
                def _():
                    copy(n, c).wait_recv()
            for m in range(STEP):
                lon_filter(
                    halves, c * STEP + m, rate_ref, scale_ref, x_ref, before_lon, after_lon,
                    y_ref, first_lat, last_lat,
                )
            for n in range(2, 4):
                @pl.when(exists[n])
                def _():
                    copy(n, c).start()

        @pl.when(c >= LAG)
        def _():
            done = c - LAG
            for n in range(2, 4):
                @pl.when(exists[n ^ 1])
                def _():
                    copy(n, done).wait_recv()
            for m in range(STEP):
                lat_filter(
                    done * STEP + m, rate_ref, scale_ref, y_ref, before_lat, after_lat, out_ref
                )

    for n in range(4):
        @pl.when(exists[n])
        def _():
            @pl.loop(0, chunks)
            def _(c):
                copy(n, c).wait_send()

    @pl.loop(1, size[0])
    def _(p):
        parcel(p).wait()


def observe_kernel(lon, rows_ref, counts_ref, cols_ref, field_ref, normal_ref, offset_ref,
                   picked_ref, collected_ref, table, values):
    modes = normal_ref.shape[0]
    owners, slots = cols_ref.shape

    def to_table(i, carry):
        slab = jnp.concatenate(
            [field_ref[0, pl.ds(i, modes, stride=lon), :], field_ref[1, pl.ds(i, modes, stride=lon), :]],
            axis=0,
        )
        table[pl.ds(pl.multiple_of(i * LANES, LANES), LANES), :] = slab.T
        return carry

    lax.fori_loop(0, lon, to_table, 0, unroll=2)

    def pick(n, carry):
        for u in range(16):
            s = n * 16 + u
            values[pl.ds(s, 1), :] = table[pl.ds(rows_ref[s], 1), :]
        return carry

    lax.fori_loop(0, owners * slots // 16, pick, 0)
    table[...] = jnp.zeros_like(table)
    slot = lax.broadcasted_iota(jnp.int32, (modes, slots), 1)

    def respond(o, carry):
        at = pl.ds(pl.multiple_of(o * slots, slots), slots)
        both = values[at, :].T
        upper = (cols_ref[pl.ds(o, 1), :] & LANES) != 0
        picked = jnp.where(upper, both[modes:], both[:modes])
        count = counts_ref[o]
        picked_ref[o, :modes] = picked
        picked_ref[o, modes:] = jnp.full((8, slots), count.astype(jnp.float32))
        adjoint = jnp.dot(
            normal_ref[...], picked, precision=HIGHEST, preferred_element_type=jnp.float32
        ) - offset_ref[o]
        adjoint = jnp.where(slot < count, adjoint, 0.0)
        values[at, :] = jnp.concatenate(
            [jnp.where(upper, 0.0, adjoint), jnp.where(upper, adjoint, 0.0)], axis=0
        ).T
        return carry

    lax.fori_loop(0, owners, respond, 0)

    def collect(n, carry):
        for u in range(16):
            s = n * 16 + u
            row = rows_ref[s]
            table[pl.ds(row, 1), :] = table[pl.ds(row, 1), :] + values[pl.ds(s, 1), :]
        return carry

    lax.fori_loop(0, owners * slots // 16, collect, 0)

    def from_table(i, carry):
        slab = table[pl.ds(pl.multiple_of(i * LANES, LANES), LANES), :].T
        collected_ref[0, pl.ds(i, modes, stride=lon), :] = slab[:modes]
        collected_ref[1, pl.ds(i, modes, stride=lon), :] = slab[modes:]
        return carry

    lax.fori_loop(0, lon, from_table, 0, unroll=2)


SMEM = pl.BlockSpec(memory_space=pltpu.SMEM)


WHOLE = pl.BlockSpec(memory_space=pltpu.VMEM)


def smooth(x, parcel, rate, scale, shape):
    modes, lon, lat = shape
    halves = x.ndim == 4
    landing = (lat // LANES, modes, REACH, LANES) if halves else (modes, REACH, lat)
    out_shape = shape if halves else (lat // LANES, modes, lon, LANES)
    return pl.pallas_call(
        functools.partial(smooth_kernel, halves),
        in_specs=[SMEM, SMEM, WHOLE, WHOLE],
        out_specs=[WHOLE, WHOLE],
        out_shape=[
            jax.ShapeDtypeStruct(out_shape, jnp.float32),
            jax.ShapeDtypeStruct(parcel.shape, jnp.float32),
        ],
        scratch_shapes=[pltpu.VMEM(shape, jnp.float32)]
        + [pltpu.VMEM(landing, jnp.float32)] * 2
        + [pltpu.VMEM((modes, 8, LANES), jnp.float32)] * 4
        + [pltpu.SemaphoreType.DMA((4, modes // STEP))] * 2
        + [pltpu.SemaphoreType.DMA((parcel.shape[0],))] * 2,
        compiler_params=pltpu.CompilerParams(
            vmem_limit_bytes=VMEM_BYTES, collective_id=int(halves), has_side_effects=True
        ),
        name="smooth_back" if halves else "smooth",
    )(rate, scale, x, parcel)


def shards(control, length_scale, modes, jacobian, obs_weight, departures, send_cols, counts):
    owners = lax.axis_size("wide")
    shape = control.shape
    mode_count, lon, lat = shape
    channels = jacobian.shape[0]
    slots = send_cols.shape[-1]
    tiles = lat // LANES

    offsets = jnp.arange(-HALO, HALO + 1).astype(jnp.float32)
    total = jnp.sum(jnp.exp(-(offsets[None, :] ** 2) / length_scale[:, None] ** 2), axis=1)
    rate = -0.5 / (length_scale * length_scale)
    scale = 1.0 / jnp.sqrt(total)

    forward = jnp.dot(jacobian, modes, precision=HIGHEST)
    weighted = obs_weight[:, None] * forward
    normal = jnp.dot(forward.T, weighted, precision=HIGHEST)
    observed = departures.reshape(owners, channels, slots)
    projected = jnp.einsum("cm,sck->smk", weighted, observed, precision=HIGHEST)

    columns = send_cols.reshape(owners, slots)
    rows = ((columns // lat) * LANES + columns % LANES).reshape(-1)

    smoothed, offset = smooth(control, projected, rate, scale, shape)
    smoothed = smoothed.reshape(tiles, mode_count * lon, LANES)
    outgoing, collected = pl.pallas_call(
        functools.partial(observe_kernel, lon),
        in_specs=[SMEM, SMEM] + [WHOLE] * 4,
        out_specs=[WHOLE, WHOLE],
        out_shape=[
            jax.ShapeDtypeStruct((owners, mode_count + 8, slots), jnp.float32),
            jax.ShapeDtypeStruct((tiles, mode_count * lon, LANES), jnp.float32),
        ],
        scratch_shapes=[
            pltpu.VMEM((lon * LANES, LANES), jnp.float32),
            pltpu.VMEM((owners * slots, LANES), jnp.float32),
        ],
        compiler_params=pltpu.CompilerParams(vmem_limit_bytes=VMEM_BYTES),
        name="observe",
    )(rows, counts.reshape(owners), columns, smoothed, normal, offset)

    response, arrived = smooth(
        collected.reshape(tiles, mode_count, lon, LANES), outgoing, rate, scale, shape
    )
    gradient = control + response

    evolved = jnp.einsum("cm,smk->sck", forward, arrived[:, :mode_count], precision=HIGHEST)
    live = jnp.arange(slots).astype(jnp.float32) < arrived[:, mode_count, :]
    residual = jnp.where(
        live[:, None, :], obs_weight[None, :, None] * (evolved - observed), jnp.float32(0.0)
    )
    return (gradient, residual.reshape(departures.shape))


def solution(mesh):
    in_specs = (
        P(None, "wide", "narrow"),
        P(),
        P(),
        P(),
        P(),
        P("wide", "narrow", None, None, None),
        P("wide", "narrow", None, None),
        P("wide", "narrow", None),
    )
    out_specs = (P(None, "wide", "narrow"), P("wide", "narrow", None, None, None))
    return jax.shard_map(shards, mesh=mesh, in_specs=in_specs, out_specs=out_specs, check_vma=False)
```

```python
import functools

import jax
import jax.numpy as jnp
from jax import lax
from jax.experimental import pallas as pl
from jax.experimental.pallas import tpu as pltpu
from jax.sharding import PartitionSpec as P

HALO = 15
REACH = 16
LANES = 128
STEP = 8
LAG = 2
HIGHEST = lax.Precision.HIGHEST
VMEM_BYTES = 24 * 2**20


def split(x):
    high = x.astype(jnp.bfloat16)
    return high, (x - high.astype(jnp.float32)).astype(jnp.bfloat16)


def taps(offset, rate, scale):
    curve = jnp.exp((offset * offset).astype(jnp.float32) * rate) * scale
    return jnp.where(jnp.abs(offset) <= HALO, curve, 0.0)


def lon_filter(halves, mode, rate_ref, scale_ref, x_ref, before_ref, after_ref, y_ref, first_ref, last_ref):
    lon = y_ref.shape[1]
    depth = lon + 2 * REACH
    row = lax.broadcasted_iota(jnp.int32, (lon, depth), 0)
    col = lax.broadcasted_iota(jnp.int32, (lon, depth), 1)
    offset = col - REACH - row
    lane = lax.broadcasted_iota(jnp.int32, (8, LANES), 1)
    if halves:
        x, before, after = (
            jnp.concatenate([ref[0, mode], ref[1, mode]], axis=1)
            for ref in (x_ref, before_ref, after_ref)
        )
    else:
        x, before, after = x_ref[mode], before_ref[mode], after_ref[mode]
    high, low = split(jnp.concatenate([before, x, after], axis=0))
    w_high, w_low = split(taps(offset, rate_ref[mode], scale_ref[mode]))
    both = jnp.dot(
        jnp.concatenate([w_high, w_low], axis=0), high, preferred_element_type=jnp.float32
    )
    y = both[:lon] + both[lon:]
    y = y + jnp.dot(w_high, low, preferred_element_type=jnp.float32)
    y_ref[mode] = y
    width = y.shape[1]
    first = jnp.zeros((8, LANES), jnp.float32)
    last = jnp.zeros((8, LANES), jnp.float32)
    for g in range(lon // 8):
        here = lane // REACH == g
        start = y[8 * g : 8 * g + 8, :LANES]
        end = y[8 * g : 8 * g + 8, width - LANES :]
        if g:
            start = pltpu.roll(start, REACH * g, 1)
        if g < 7:
            end = pltpu.roll(end, REACH * g + REACH, 1)
        first = jnp.where(here, start, first)
        last = jnp.where(here, end, last)
    first_ref[mode] = first
    last_ref[mode] = last


def lat_filter(mode, rate_ref, scale_ref, y_ref, before_ref, after_ref, out_ref):
    lon, lat = y_ref.shape[1], y_ref.shape[2]
    tiles = lat // LANES
    depth = 2 * LANES
    row = lax.broadcasted_iota(jnp.int32, (depth, LANES), 0)
    col = lax.broadcasted_iota(jnp.int32, (depth, LANES), 1)
    offset = jnp.where(row < 3 * LANES // 2, row, row - depth) - col
    near = lax.broadcasted_iota(jnp.int32, (lon, LANES), 1) < LANES // 2
    before, after = before_ref[mode], after_ref[mode]
    lefts, rights = [], []
    for g in range(lon // 8):
        lefts.append(pltpu.roll(before, LANES - REACH - REACH * g, 1) if g < 7 else before)
        rights.append(pltpu.roll(after, LANES - REACH * g, 1) if g else after)
    blocks = [y_ref[mode, :, LANES * t : LANES * t + LANES] for t in range(tiles)]
    around = [jnp.concatenate(lefts, axis=0)] + blocks + [jnp.concatenate(rights, axis=0)]
    sides = [jnp.where(near, around[t + 2], around[t]) for t in range(tiles)]
    field = jnp.concatenate(
        [jnp.concatenate([blocks[t], sides[t]], axis=1) for t in range(tiles)], axis=0
    )
    high, low = split(field)
    w_high, w_low = split(taps(offset, rate_ref[mode], scale_ref[mode]))
    both = jnp.dot(
        jnp.concatenate([high, low], axis=0),
        jnp.concatenate([w_high, w_low], axis=1),
        preferred_element_type=jnp.float32,
    )
    count = tiles * lon
    z = both[:count, :LANES] + both[:count, LANES:] + both[count:, :LANES]
    for t in range(tiles):
        part = z[lon * t : lon * t + lon]
        if len(out_ref.shape) == 3:
            out_ref[mode, :, LANES * t : LANES * t + LANES] = part
        else:
            out_ref[t, mode] = part


def smooth_kernel(halves, rate_ref, scale_ref, x_ref, parcel_ref, out_ref, arrived_ref, y_ref,
                  before_lon, after_lon, first_lat, last_lat, before_lat, after_lat,
                  send_sems, recv_sems, parcel_send, parcel_recv):
    modes, lon = y_ref.shape[0], y_ref.shape[1]
    chunks = modes // STEP
    axes = ("wide", "narrow")
    spot = [lax.axis_index(axis) for axis in axes]
    size = [lax.axis_size(axis) for axis in axes]
    exists = [spot[0] > 0, spot[0] < size[0] - 1, spot[1] > 0, spot[1] < size[1] - 1]
    target = [{axes[n // 2]: spot[n // 2] + (1 if n % 2 else -1)} for n in range(4)]

    def copy(n, c):
        at = pl.ds(c * STEP, STEP)
        if n < 2:
            rows = pl.ds(lon - REACH, REACH) if n else pl.ds(0, REACH)
            landing = before_lon if n else after_lon
            src = x_ref.at[:, at, rows] if halves else x_ref.at[at, rows]
            dst = landing.at[:, at] if halves else landing.at[at]
        else:
            src = (last_lat if n == 3 else first_lat).at[at]
            dst = (before_lat if n == 3 else after_lat).at[at]
        return pltpu.make_async_remote_copy(
            src_ref=src,
            dst_ref=dst,
            send_sem=send_sems.at[n, c],
            recv_sem=recv_sems.at[n, c],
            device_id=target[n],
            device_id_type=pl.DeviceIdType.MESH,
        )

    def parcel(p):
        peer = lax.rem(spot[0] + p, size[0])
        return pltpu.make_async_remote_copy(
            src_ref=parcel_ref.at[peer],
            dst_ref=arrived_ref.at[spot[0]],
            send_sem=parcel_send.at[p],
            recv_sem=parcel_recv.at[p],
            device_id={"wide": peer},
            device_id_type=pl.DeviceIdType.MESH,
        )

    barrier = pltpu.get_barrier_semaphore()

    @pl.loop(1, size[0])
    def _(p):
        pl.semaphore_signal(
            barrier, inc=1, device_id={"wide": lax.rem(spot[0] + p, size[0])},
            device_id_type=pl.DeviceIdType.MESH,
        )
    for n in range(2, 4):
        @pl.when(exists[n])
        def _():
            pl.semaphore_signal(
                barrier, inc=1, device_id=target[n], device_id_type=pl.DeviceIdType.MESH
            )
    pl.semaphore_wait(barrier, size[0] - 1 + sum(there.astype(jnp.int32) for there in exists[2:]))

    for n in range(2):
        @pl.when(exists[n])
        def _():
            @pl.loop(0, chunks)
            def _(c):
                copy(n, c).start()

    @pl.loop(1, size[0])
    def _(p):
        parcel(p).start()

    arrived_ref[spot[0]] = parcel_ref[spot[0]]

    for n, landing in ((1, before_lon), (0, after_lon), (3, before_lat), (2, after_lat)):
        @pl.when(jnp.logical_not(exists[n ^ 1]))
        def _():
            landing[...] = jnp.zeros_like(landing)

    @pl.loop(0, chunks + LAG)
    def _(c):
        @pl.when(c < chunks)
        def _():
            for n in range(2):
                @pl.when(exists[n ^ 1])
                def _():
                    copy(n, c).wait_recv()
            for m in range(STEP):
                lon_filter(
                    halves, c * STEP + m, rate_ref, scale_ref, x_ref, before_lon, after_lon,
                    y_ref, first_lat, last_lat,
                )
            for n in range(2, 4):
                @pl.when(exists[n])
                def _():
                    copy(n, c).start()

        @pl.when(c >= LAG)
        def _():
            done = c - LAG
            for n in range(2, 4):
                @pl.when(exists[n ^ 1])
                def _():
                    copy(n, done).wait_recv()
            for m in range(STEP):
                lat_filter(
                    done * STEP + m, rate_ref, scale_ref, y_ref, before_lat, after_lat, out_ref
                )

    for n in range(4):
        @pl.when(exists[n])
        def _():
            @pl.loop(0, chunks)
            def _(c):
                copy(n, c).wait_send()

    @pl.loop(1, size[0])
    def _(p):
        parcel(p).wait()


def observe_kernel(lon, rows_ref, counts_ref, cols_ref, field_ref, normal_ref, offset_ref,
                   picked_ref, collected_ref, table, values):
    modes = normal_ref.shape[0]
    owners, slots = cols_ref.shape

    def to_table(i, carry):
        slab = jnp.concatenate(
            [field_ref[0, pl.ds(i, modes, stride=lon), :], field_ref[1, pl.ds(i, modes, stride=lon), :]],
            axis=0,
        )
        table[pl.ds(pl.multiple_of(i * LANES, LANES), LANES), :] = slab.T
        return carry

    lax.fori_loop(0, lon, to_table, 0, unroll=2)

    def pick(n, carry):
        for u in range(16):
            s = n * 16 + u
            values[pl.ds(s, 1), :] = table[pl.ds(rows_ref[s], 1), :]
        return carry

    lax.fori_loop(0, owners * slots // 16, pick, 0)
    table[...] = jnp.zeros_like(table)
    slot = lax.broadcasted_iota(jnp.int32, (modes, slots), 1)

    def respond(o, carry):
        at = pl.ds(pl.multiple_of(o * slots, slots), slots)
        both = values[at, :].T
        upper = (cols_ref[pl.ds(o, 1), :] & LANES) != 0
        picked = jnp.where(upper, both[modes:], both[:modes])
        count = counts_ref[o]
        picked_ref[o, :modes] = picked
        picked_ref[o, modes:] = jnp.full((8, slots), count.astype(jnp.float32))
        adjoint = jnp.dot(
            normal_ref[...], picked, precision=HIGHEST, preferred_element_type=jnp.float32
        ) - offset_ref[o]
        adjoint = jnp.where(slot < count, adjoint, 0.0)
        values[at, :] = jnp.concatenate(
            [jnp.where(upper, 0.0, adjoint), jnp.where(upper, adjoint, 0.0)], axis=0
        ).T
        return carry

    lax.fori_loop(0, owners, respond, 0)

    def collect(n, carry):
        for u in range(16):
            s = n * 16 + u
            row = rows_ref[s]
            table[pl.ds(row, 1), :] = table[pl.ds(row, 1), :] + values[pl.ds(s, 1), :]
        return carry

    lax.fori_loop(0, owners * slots // 16, collect, 0)

    def from_table(i, carry):
        slab = table[pl.ds(pl.multiple_of(i * LANES, LANES), LANES), :].T
        collected_ref[0, pl.ds(i, modes, stride=lon), :] = slab[:modes]
        collected_ref[1, pl.ds(i, modes, stride=lon), :] = slab[modes:]
        return carry

    lax.fori_loop(0, lon, from_table, 0, unroll=2)


SMEM = pl.BlockSpec(memory_space=pltpu.SMEM)


WHOLE = pl.BlockSpec(memory_space=pltpu.VMEM)


def smooth(x, parcel, rate, scale, shape):
    modes, lon, lat = shape
    halves = x.ndim == 4
    landing = (lat // LANES, modes, REACH, LANES) if halves else (modes, REACH, lat)
    out_shape = shape if halves else (lat // LANES, modes, lon, LANES)
    return pl.pallas_call(
        functools.partial(smooth_kernel, halves),
        in_specs=[SMEM, SMEM, WHOLE, WHOLE],
        out_specs=[WHOLE, WHOLE],
        out_shape=[
            jax.ShapeDtypeStruct(out_shape, jnp.float32),
            jax.ShapeDtypeStruct(parcel.shape, jnp.float32),
        ],
        scratch_shapes=[pltpu.VMEM(shape, jnp.float32)]
        + [pltpu.VMEM(landing, jnp.float32)] * 2
        + [pltpu.VMEM((modes, 8, LANES), jnp.float32)] * 4
        + [pltpu.SemaphoreType.DMA((4, modes // STEP))] * 2
        + [pltpu.SemaphoreType.DMA((parcel.shape[0],))] * 2,
        compiler_params=pltpu.CompilerParams(
            vmem_limit_bytes=VMEM_BYTES, collective_id=int(halves), has_side_effects=True
        ),
        name="smooth_back" if halves else "smooth",
    )(rate, scale, x, parcel)


def add_kernel(a_ref, b_ref, out_ref):
    out_ref[...] = a_ref[...] + b_ref[...]


def plus(a, b):
    block = pl.BlockSpec((STEP,) + a.shape[1:], lambda g: (g, 0, 0))
    return pl.pallas_call(
        add_kernel,
        grid=(a.shape[0] // STEP,),
        in_specs=[block, block],
        out_specs=block,
        out_shape=jax.ShapeDtypeStruct(a.shape, a.dtype),
        compiler_params=pltpu.CompilerParams(vmem_limit_bytes=VMEM_BYTES),
        name="plus",
    )(a, b)


def shards(control, length_scale, modes, jacobian, obs_weight, departures, send_cols, counts):
    owners = lax.axis_size("wide")
    shape = control.shape
    mode_count, lon, lat = shape
    channels = jacobian.shape[0]
    slots = send_cols.shape[-1]
    tiles = lat // LANES

    offsets = jnp.arange(-HALO, HALO + 1).astype(jnp.float32)
    total = jnp.sum(jnp.exp(-(offsets[None, :] ** 2) / length_scale[:, None] ** 2), axis=1)
    rate = -0.5 / (length_scale * length_scale)
    scale = 1.0 / jnp.sqrt(total)

    forward = jnp.dot(jacobian, modes, precision=HIGHEST)
    weighted = obs_weight[:, None] * forward
    normal = jnp.dot(forward.T, weighted, precision=HIGHEST)
    observed = departures.reshape(owners, channels, slots)
    projected = jnp.einsum("cm,sck->smk", weighted, observed, precision=HIGHEST)

    columns = send_cols.reshape(owners, slots)
    rows = ((columns // lat) * LANES + columns % LANES).reshape(-1)

    smoothed, offset = smooth(control, projected, rate, scale, shape)
    smoothed = smoothed.reshape(tiles, mode_count * lon, LANES)
    outgoing, collected = pl.pallas_call(
        functools.partial(observe_kernel, lon),
        in_specs=[SMEM, SMEM] + [WHOLE] * 4,
        out_specs=[WHOLE, WHOLE],
        out_shape=[
            jax.ShapeDtypeStruct((owners, mode_count + 8, slots), jnp.float32),
            jax.ShapeDtypeStruct((tiles, mode_count * lon, LANES), jnp.float32),
        ],
        scratch_shapes=[
            pltpu.VMEM((lon * LANES, LANES), jnp.float32),
            pltpu.VMEM((owners * slots, LANES), jnp.float32),
        ],
        compiler_params=pltpu.CompilerParams(vmem_limit_bytes=VMEM_BYTES),
        name="observe",
    )(rows, counts.reshape(owners), columns, smoothed, normal, offset)

    response, arrived = smooth(
        collected.reshape(tiles, mode_count, lon, LANES), outgoing, rate, scale, shape
    )
    gradient = plus(control, response)

    evolved = jnp.einsum("cm,smk->sck", forward, arrived[:, :mode_count], precision=HIGHEST)
    live = jnp.arange(slots).astype(jnp.float32) < arrived[:, mode_count, :]
    residual = jnp.where(
        live[:, None, :], obs_weight[None, :, None] * (evolved - observed), jnp.float32(0.0)
    )
    return (gradient, residual.reshape(departures.shape))


def solution(mesh):
    in_specs = (
        P(None, "wide", "narrow"),
        P(),
        P(),
        P(),
        P(),
        P("wide", "narrow", None, None, None),
        P("wide", "narrow", None, None),
        P("wide", "narrow", None),
    )
    out_specs = (P(None, "wide", "narrow"), P("wide", "narrow", None, None, None))
    return jax.shard_map(shards, mesh=mesh, in_specs=in_specs, out_specs=out_specs, check_vma=False)
```
